32 devices in a mesh: loop: 4 (over z), grp: 8 (over y, x, core).
Axes of the slice: x: 2, y: 2, z: 4, core: 2. Of those that a mesh axis runs over, the one named last changes fastest.
Arguments:
- images: bfloat16 [4096, 1152], P(('loop', 'grp')), may hold values from -0.1796875 to 0.1796875
- texts: bfloat16 [4096, 1152], P(('loop', 'grp')), may hold values from -0.1796875 to 0.1796875
- log_scale: float32 [], replicated, may hold values from 1.6 to 2.6
- bias: float32 [], replicated, may hold values from -6 to -2
Outputs:
- image_grad: float32 [4096, 1152], P(('loop', 'grp'))
- text_grad: float32 [4096, 1152], P(('loop', 'grp'))
The draws below stay inside these ranges and needn't reach their ends.
All inputs are finite; a program needn't handle non-finite values.
Results may differ from the reference program's by a relative error of at most 0.0045.
Values may be sent and summed in bfloat16 or wider, within the bound.
A program may use at most 64 MiB of HBM per device.

```python
import jax
import jax.numpy as jnp
from jax import lax

D = 1152
ROWS_DEV = 128
WIN = 8
BATCH = 4096
N_LOOP = 4
N_GRP = 8


def block_scale(key, shape, split, low, largest):
    factor_of, own = 1.0, jax.random.fold_in(key, 6)
    for dim, parts in split:
        draws = jnp.exp(jax.random.uniform(jax.random.fold_in(own, dim), (parts,), jnp.float32, low / len(split), largest / len(split)))
        factor_of = factor_of * jnp.repeat(draws, shape[dim] // parts).reshape([-1 if axis == dim else 1 for axis in range(len(shape))])
    return factor_of


def normal_values(own_key, shape, spread, most, shards=(), held_as=jnp.bfloat16):
    entries = spread * jax.random.normal(own_key, shape, jnp.float32)
    if shards:
        entries = entries * block_scale(own_key, shape, shards, -0.22, 0.18)
    return jnp.clip(entries, -most, most).astype(held_as)


def setup_inputs(seed: int = 0) -> dict:
    splits = jax.random.split(jax.random.key(seed), 5)
    return {
        "images": normal_values(splits[0], (BATCH, D), 0.03, 0.1796875, ((0, 32),)),
        "texts": normal_values(splits[1], (BATCH, D), 0.03, 0.1796875, ((0, 32),)),
        "log_scale": jnp.clip(jax.random.uniform(splits[2], (), jnp.float32, 1.6, 2.6), 1.6, 2.6),
        "bias": jnp.clip(jax.random.uniform(splits[3], (), jnp.float32, -6.0, -2.0), -6.0, -2.0),
    }


def normalize(values):
    full = values.astype(jnp.float32)
    inverse = lax.rsqrt(lax.optimization_barrier(jnp.sum(full * full, axis=-1, keepdims=True)) + 1e-06)
    return (full * inverse, inverse)

def unnormalize(unit, inverse, grad):
    return inverse * (grad - unit * lax.optimization_barrier(jnp.sum(unit * grad, axis=-1, keepdims=True)))

def tile_terms(rolled, image_bf, scale, bias, sign):
    logits = jnp.einsum('jkd,jid->jki', rolled, image_bf)
    level = scale * logits + bias
    weights = (scale * -sign * jax.nn.sigmoid(-sign * level)).astype(jnp.bfloat16).astype(jnp.float32)
    image_part = jnp.einsum('jki,jkd->jid', weights, rolled)
    text_part = jnp.einsum('jki,jid->jkd', weights, image_bf)
    return (image_part, text_part)

def reference(images, texts, log_scale, bias):
    shape = (N_LOOP * N_GRP, ROWS_DEV, D)
    image_unit, image_inv = normalize(images)
    text_unit, text_inv = normalize(texts)
    image_bf = image_unit.astype(jnp.bfloat16).astype(jnp.float32).reshape(shape)
    text_bf = text_unit.astype(jnp.bfloat16).astype(jnp.float32).reshape(shape)
    scale = jnp.exp(log_scale)
    matched = jnp.eye(ROWS_DEV, dtype=jnp.float32)
    own_sign = (2.0 * matched - 1.0)[None]
    other_sign = jnp.float32(-1.0)
    image_acc = jnp.zeros(shape, jnp.float32)
    text_acc = jnp.zeros(shape, jnp.float32)
    for offset in range(WIN):
        rolled = jnp.roll(text_bf, offset, axis=0)
        sign = own_sign if offset == 0 else other_sign
        image_part, text_part = tile_terms(rolled, image_bf, scale, bias, sign)
        image_acc = image_acc + image_part
        text_acc = text_acc + jnp.roll(text_part, -offset, axis=0)
    image_grad = unnormalize(image_unit, image_inv, image_acc.reshape(BATCH, D))
    text_grad = unnormalize(text_unit, text_inv, text_acc.reshape(BATCH, D))
    return (image_grad, text_grad)
```

```python
import functools

import jax
import jax.numpy as jnp
from jax import lax
from jax.experimental import pallas as pl
from jax.experimental.pallas import tpu as pltpu
from jax.sharding import PartitionSpec as P

WIN = 8
MESH = pl.DeviceIdType.MESH
NT = (((1,), (1,)), ((), ()))


def kernel(
    n_loop, n_grp, images_ref, texts_ref, log_scale_ref, bias_ref, image_grad_ref, text_grad_ref,
    own, held, acc, send_sem, pass_sem, recv_sem,
):
    n = n_loop * n_grp
    me = lax.axis_index("loop") * n_grp + lax.axis_index("grp")
    core = lax.rem(me, 2)

    def place(steps):
        device = lax.rem(me + steps + n, n)
        return (device // n_grp, lax.rem(device, n_grp))

    sibling = place(1 - 2 * core)
    far = place(14 * core - 7)
    barrier = pltpu.get_barrier_semaphore()
    peers = [place(s) for s in (-6, -4, -2, 2, 4, 6)] + [sibling, far]
    for peer in peers:
        pl.semaphore_signal(barrier, inc=1, device_id=peer, device_id_type=MESH)

    def normalize(ref):
        full = ref[...].astype(jnp.float32)
        inverse = lax.rsqrt(jnp.sum(full * full, axis=-1, keepdims=True) + 1e-06)
        return full * inverse, inverse

    own[0] = normalize(texts_ref)[0].astype(jnp.bfloat16)
    own[1] = normalize(images_ref)[0].astype(jnp.bfloat16)
    pl.semaphore_wait(barrier, len(peers))

    def copy(source, kind, slot, send, device):
        return pltpu.make_async_remote_copy(
            src_ref=source, dst_ref=held.at[kind, slot], send_sem=send,
            recv_sem=recv_sem.at[kind, slot], device_id=device, device_id_type=MESH,
        )

    sends = []
    for j in (3, 2, 1):
        for kind, way in ((0, 1), (1, -1)):
            sends.append(copy(own.at[kind], kind, 2 * j - 1, send_sem.at[kind, j], place(way * 2 * j)))
    up = place(1 + 6 * core)
    down = place(-7 + 6 * core)
    sends.append(copy(own.at[0], 0, 6 * core, send_sem.at[0, 0], up))
    sends.append(copy(own.at[1], 1, 6 - 6 * core, send_sem.at[1, 0], down))
    for one in sends:
        one.start()

    scale = jnp.exp(jnp.full((1, 128), log_scale_ref[0], jnp.float32))
    bias = bias_ref[0]

    def step(kind, block, matched):
        logits = lax.dot_general(own[1 - kind], block, NT, preferred_element_type=jnp.float32)
        level = scale * logits + bias
        if matched:
            rows = lax.broadcasted_iota(jnp.int32, level.shape, 0)
            columns = lax.broadcasted_iota(jnp.int32, level.shape, 1)
            sign = jnp.where(rows == columns, 1.0, -1.0)
            weights = scale * -sign * jax.nn.sigmoid(-sign * level)
        else:
            weights = scale * jax.nn.sigmoid(level)
        part = jnp.dot(weights.astype(jnp.bfloat16), block, preferred_element_type=jnp.float32)
        acc[kind] = part if matched else acc[kind] + part

    for kind in range(2):
        step(kind, own[kind], True)

    passes = []
    for j in (1, 2, 3):
        for kind in range(2):
            copy(own.at[kind], kind, 2 * j - 1, send_sem.at[kind, j], sibling).wait_recv()
            lean = core if kind == 0 else 1 - core
            one = copy(held.at[kind, 2 * j - 1], kind, 2 * j - 2 * lean, pass_sem.at[kind, j - 1], sibling)
            one.start()
            passes.append(one)
            step(kind, held[kind, 2 * j - 1], False)
    for slot in (0, 2, 4, 6):
        for kind in range(2):
            copy(own.at[kind], kind, slot, send_sem.at[kind, 0], sibling).wait_recv()
            step(kind, held[kind, slot], False)

    for source, kind, out in ((images_ref, 0, image_grad_ref), (texts_ref, 1, text_grad_ref)):
        unit, inverse = normalize(source)
        grad = acc[kind]
        out[...] = inverse * (grad - unit * jnp.sum(unit * grad, axis=-1, keepdims=True))
    for one in sends + passes:
        one.wait_send()


def per_device(n_loop, n_grp, images, texts, log_scale, bias):
    rows, width = images.shape
    vmem = pl.BlockSpec(memory_space=pltpu.VMEM)
    smem = pl.BlockSpec(memory_space=pltpu.SMEM)
    grad = jax.ShapeDtypeStruct((rows, width), jnp.float32)
    return pl.pallas_call(
        functools.partial(kernel, n_loop, n_grp),
        out_shape=(grad, grad),
        in_specs=[vmem, vmem, smem, smem],
        out_specs=(vmem, vmem),
        scratch_shapes=[
            pltpu.VMEM((2, rows, width), jnp.bfloat16),
            pltpu.VMEM((2, WIN - 1, rows, width), jnp.bfloat16),
            pltpu.VMEM((2, rows, width), jnp.float32),
            pltpu.SemaphoreType.DMA((2, 4)),
            pltpu.SemaphoreType.DMA((2, 3)),
            pltpu.SemaphoreType.DMA((2, WIN - 1)),
        ],
        compiler_params=pltpu.CompilerParams(
            collective_id=0, has_side_effects=True, vmem_limit_bytes=32 * 1024 * 1024
        ),
    )(images, texts, log_scale.reshape(1), bias.reshape(1))


def solution(mesh):
    rows = P(("loop", "grp"), None)
    return jax.shard_map(
        functools.partial(per_device, mesh.shape["loop"], mesh.shape["grp"]),
        mesh=mesh,
        in_specs=(rows, rows, P(), P()),
        out_specs=(rows, rows),
        check_vma=False,
    )
```

```python
import functools

import jax
import jax.numpy as jnp
from jax import lax
from jax.experimental import pallas as pl
from jax.experimental.pallas import tpu as pltpu
from jax.sharding import PartitionSpec as P

WIN = 8
MESH = pl.DeviceIdType.MESH
NT = (((1,), (1,)), ((), ()))


def kernel(
    n_loop, n_grp, images_hbm, texts_hbm, log_scale_ref, bias_ref, image_grad_ref, text_grad_ref,
    raw, own, crossed, held, acc, load_sem, cross_send, cross_recv, send_sem, pass_sem, recv_sem,
):
    n = n_loop * n_grp
    me = lax.axis_index("loop") * n_grp + lax.axis_index("grp")
    bits = [lax.rem(me, 2), lax.rem(me // 2, 2), lax.rem(me // 4, 2)]
    top = [None] + [bits[r.bit_length() - 1] for r in range(1, WIN)]

    def place(device):
        return (device // n_grp, lax.rem(device, n_grp))

    def member(r):
        device = me
        for b in range(3):
            if r >> b & 1:
                device = device + (1 - 2 * bits[b]) * (1 << b)
        return place(device)

    above, below = place(lax.rem(me + WIN, n)), place(lax.rem(me - WIN + n, n))
    loads = [
        pltpu.make_async_copy(ref, raw.at[i], load_sem.at[i]) for i, ref in enumerate((texts_hbm, images_hbm))
    ]
    for one in loads:
        one.start()
    barrier = pltpu.get_barrier_semaphore()
    peers = [above, below] + [member(r) for r in (1, 2, 4, 6)]
    for peer in peers:
        pl.semaphore_signal(barrier, inc=1, device_id=peer, device_id_type=MESH)

    def normalize(kind):
        full = raw[kind].astype(jnp.float32)
        inverse = lax.rsqrt(jnp.sum(full * full, axis=-1, keepdims=True) + 1e-06)
        return full * inverse, inverse

    for kind in range(2):
        loads[kind].wait()
        own[kind] = normalize(kind)[0].astype(jnp.bfloat16)
    pl.semaphore_wait(barrier, len(peers))

    def send(source, late, r, sem, device):
        return pltpu.make_async_remote_copy(
            src_ref=source, dst_ref=held.at[late, r - 1], send_sem=sem,
            recv_sem=recv_sem.at[late, r - 1], device_id=device, device_id_type=MESH,
        )

    crosses = [
        pltpu.make_async_remote_copy(
            src_ref=own.at[kind], dst_ref=crossed.at[kind], send_sem=cross_send.at[kind],
            recv_sem=cross_recv.at[kind], device_id=device, device_id_type=MESH,
        )
        for kind, device in ((0, above), (1, below))
    ]
    near = [send(own.at[top[r]], 0, r, send_sem.at[0, r - 1], member(r)) for r in (1, 2, 4, 6)]
    late = [send(crossed.at[1 - top[r]], 1, r, send_sem.at[1, r - 1], member(r)) for r in (1, 2, 4, 6)]
    for one in crosses + near:
        one.start()

    scale = jnp.exp(jnp.full((1, 128), log_scale_ref[0], jnp.float32))
    bias = bias_ref[0]

    def step(kind, block, matched=False):
        logits = lax.dot_general(own[1 - kind], block, NT, preferred_element_type=jnp.float32)
        level = scale * logits + bias
        if matched:
            rows = lax.broadcasted_iota(jnp.int32, level.shape, 0)
            columns = lax.broadcasted_iota(jnp.int32, level.shape, 1)
            sign = jnp.where(rows == columns, 1.0, -1.0)
            weights = scale * -sign * jax.nn.sigmoid(-sign * level)
        else:
            weights = scale * jax.nn.sigmoid(level)
        part = jnp.dot(weights.astype(jnp.bfloat16), block, preferred_element_type=jnp.float32)
        acc[kind] = part if matched else acc[kind] + part

    for kind in range(2):
        step(kind, own[kind], True)

    passes = []

    def arrived(is_late, r):
        send(own.at[0], is_late, r, send_sem.at[is_late, r - 1], member(1)).wait_recv()
        if r in (2, 4, 6):
            one = send(held.at[is_late, r - 1], is_late, r + 1, pass_sem.at[is_late, r // 2 - 1], member(1))
            one.start()
            passes.append(one)
        step(top[r] if is_late else 1 - top[r], held[is_late, r - 1])

    for r in (1, 2, 4):
        arrived(0, r)
    for one in crosses:
        one.wait_recv()
    for one in late:
        one.start()
    for r in (6, 3, 5, 7):
        arrived(0, r)
    for r in (1, 2, 4, 6, 3, 5, 7):
        arrived(1, r)

    for kind, out in ((1, image_grad_ref), (0, text_grad_ref)):
        unit, inverse = normalize(kind)
        grad = acc[1 - kind]
        out[...] = inverse * (grad - unit * jnp.sum(unit * grad, axis=-1, keepdims=True))
    for one in crosses + near + late + passes:
        one.wait_send()


def per_device(n_loop, n_grp, images, texts, log_scale, bias):
    rows, width = images.shape
    vmem = pl.BlockSpec(memory_space=pltpu.VMEM)
    smem = pl.BlockSpec(memory_space=pltpu.SMEM)
    hbm = pl.BlockSpec(memory_space=pl.ANY)
    grad = jax.ShapeDtypeStruct((rows, width), jnp.float32)
    dma = pltpu.SemaphoreType.DMA
    return pl.pallas_call(
        functools.partial(kernel, n_loop, n_grp),
        out_shape=(grad, grad),
        in_specs=[hbm, hbm, smem, smem],
        out_specs=(vmem, vmem),
        scratch_shapes=[
            pltpu.VMEM((2, rows, width), jnp.bfloat16),
            pltpu.VMEM((2, rows, width), jnp.bfloat16),
            pltpu.VMEM((2, rows, width), jnp.bfloat16),
            pltpu.VMEM((2, WIN - 1, rows, width), jnp.bfloat16),
            pltpu.VMEM((2, rows, width), jnp.float32),
            dma((2,)),
            dma((2,)),
            dma((2,)),
            dma((2, WIN - 1)),
            dma((2, 3)),
            dma((2, WIN - 1)),
        ],
        compiler_params=pltpu.CompilerParams(
            collective_id=0, has_side_effects=True, vmem_limit_bytes=48 * 1024 * 1024
        ),
    )(images, texts, log_scale.reshape(1), bias.reshape(1))


def solution(mesh):
    rows = P(("loop", "grp"), None)
    return jax.shard_map(
        functools.partial(per_device, mesh.shape["loop"], mesh.shape["grp"]),
        mesh=mesh,
        in_specs=(rows, rows, P(), P()),
        out_specs=(rows, rows),
        check_vma=False,
    )
```

```python
import functools

import jax
import jax.numpy as jnp
from jax import lax
from jax.experimental import pallas as pl
from jax.experimental.pallas import tpu as pltpu
from jax.sharding import PartitionSpec as P

WIN = 8
CHUNKS = 3
SIZES = (2, 2, 2, 2)
PARTS = len(SIZES)
ROUTES = ('CDDY', 'CDDY')
MESH = pl.DeviceIdType.MESH
NT = (((1,), (1,)), ((), ()))


def kernel(
    n_loop, n_grp, images_hbm, texts_hbm, log_scale_ref, bias_ref, image_grad_ref, text_grad_ref,
    raw, own, crossed, held, acc, load_sem, cross_send, cross_recv, send_sem, pass_sem, turn_sem, recv_sem,
):
    n = n_loop * n_grp
    wide = own.shape[2] // CHUNKS
    unit = images_hbm.shape[0] // 8
    offsets = [sum(SIZES[:h]) * unit for h in range(PARTS)]
    me = lax.axis_index("loop") * n_grp + lax.axis_index("grp")
    bits = [lax.rem(me, 2), lax.rem(me // 2, 2), lax.rem(me // 4, 2)]
    top = [None] + [bits[r.bit_length() - 1] for r in range(1, WIN)]

    def place(device):
        return (device // n_grp, lax.rem(device, n_grp))

    def member(r):
        device = me
        for b in range(3):
            if r >> b & 1:
                device = device + (1 - 2 * bits[b]) * (1 << b)
        return place(device)

    above, below = place(lax.rem(me + WIN, n)), place(lax.rem(me - WIN + n, n))
    loads = [
        pltpu.make_async_copy(ref, raw.at[i], load_sem.at[i]) for i, ref in enumerate((texts_hbm, images_hbm))
    ]
    for one in loads:
        one.start()
    barrier = pltpu.get_barrier_semaphore()
    peers = [above, below] + [member(r) for r in (1, 2, 4, 6)]
    for peer in peers:
        pl.semaphore_signal(barrier, inc=1, device_id=peer, device_id_type=MESH)

    def normalize(kind):
        full = raw[kind].astype(jnp.float32)
        inverse = lax.rsqrt(jnp.sum(full * full, axis=-1, keepdims=True) + 1e-06)
        return full * inverse, inverse

    for kind in range(2):
        loads[kind].wait()
        own[kind] = normalize(kind)[0].astype(jnp.bfloat16)
    pl.semaphore_wait(barrier, len(peers))

    def half(ref, h):
        return ref.at[pl.ds(offsets[h], SIZES[h] * unit)]

    def send(source, late, r, h, sem, device):
        return pltpu.make_async_remote_copy(
            src_ref=half(source, h), dst_ref=half(held.at[late, r - 1], h), send_sem=sem.at[late, r - 1, h],
            recv_sem=recv_sem.at[late, r - 1, h], device_id=device, device_id_type=MESH,
        )

    def cross(kind, h):
        return pltpu.make_async_remote_copy(
            src_ref=half(own.at[kind], h), dst_ref=half(crossed.at[kind], h), send_sem=cross_send.at[kind, h],
            recv_sem=cross_recv.at[kind, h], device_id=(above, below)[kind], device_id_type=MESH,
        )

    started = []

    def start(one):
        one.start()
        started.append(one)

    def spread(late, h):
        def block(r):
            return crossed.at[1 - top[r]] if late else own.at[top[r]]

        for r in (2, 4, 1):
            start(send(block(r), late, r, h, send_sem, member(r)))
        if ROUTES[late][h] == "C":
            start_if(send(block(6), late, 6, h, send_sem, member(6)))

    even = bits[1] * bits[2] + (1 - bits[1]) * (1 - bits[2])
    turn = place(me + even * (1 - 2 * bits[1]) * 2 + (1 - even) * (1 - 2 * bits[2]) * 4)
    started_if = []

    def start_if(one):
        @pl.when(even == 0)
        def _():
            one.start()

        started_if.append(one)

    def relay(late, h):
        route = ROUTES[late][h]
        if route == "Y":
            start(send(held.at[late, 3], late, 6, h, turn_sem, member(2)))
        elif route == "D":
            start(send(held.at[late, 1 + 2 * even], late, 6, h, turn_sem, turn))
        else:
            start_if(send(held.at[late, 1], late, 6, h, turn_sem, member(4)))

    def direct(late, h):
        for r in (2, 4):
            send(own.at[0], late, r, h, send_sem, member(1)).wait_recv()
        relay(late, h)
        for r in (2, 4):
            start(send(held.at[late, r - 1], late, r + 1, h, pass_sem, member(1)))

    scale = jnp.exp(jnp.full((1, 1), log_scale_ref[0], jnp.float32))
    bias = bias_ref[0]

    def step(kind, block, matched=False):
        def columns(ref, c):
            value = ref[..., c * wide : (c + 1) * wide]
            return value.reshape(-1, wide)

        logits = sum(
            lax.dot_general(columns(own.at[1 - kind], c), columns(block, c), NT, preferred_element_type=jnp.float32)
            for c in range(CHUNKS)
        )
        level = scale * logits + bias
        if matched:
            rows = lax.broadcasted_iota(jnp.int32, level.shape, 0)
            others = lax.broadcasted_iota(jnp.int32, level.shape, 1)
            sign = jnp.where(rows == others, 1.0, -1.0)
            weights = scale * -sign * jax.nn.sigmoid(-sign * level)
        else:
            weights = scale * jax.nn.sigmoid(level)
        weights = weights.astype(jnp.bfloat16)
        for c in range(CHUNKS):
            at = (kind, slice(None), slice(c * wide, (c + 1) * wide))
            part = jnp.dot(weights, columns(block, c), preferred_element_type=jnp.float32)
            acc[at] = part if matched else acc[at] + part

    for h in range(PARTS):
        for kind in range(2):
            start(cross(kind, h))
        spread(0, h)
    for kind in range(2):
        step(kind, own.at[kind], True)

    def arrived(late, *relations):
        for h in range(PARTS):
            for r in relations:
                send(own.at[0], late, r, h, send_sem, member(1)).wait_recv()
                if r == 6:
                    start(send(held.at[late, 5], late, 7, h, pass_sem, member(1)))

    def use(late, first, count):
        step(top[first] if late else 1 - top[first], held.at[late, pl.ds(first - 1, count)])

    def crossing(h):
        for kind in range(2):
            cross(kind, h).wait_recv()
        spread(1, h)

    arrived(0, 1)
    use(0, 1, 1)
    direct(0, 0)
    direct(0, 1)
    crossing(0)
    direct(0, 2)
    direct(0, 3)
    crossing(1)
    use(0, 2, 1)
    use(0, 4, 1)
    crossing(2)
    arrived(0, 3, 5)
    use(0, 3, 1)
    direct(1, 0)
    crossing(3)
    direct(1, 1)
    arrived(0, 6)
    direct(1, 2)
    use(0, 5, 1)
    direct(1, 3)
    arrived(1, 1)
    use(1, 1, 1)
    use(1, 2, 1)
    use(1, 4, 1)
    arrived(0, 7)
    use(0, 6, 2)
    arrived(1, 3, 5)
    arrived(1, 6)
    use(1, 3, 1)
    use(1, 5, 1)
    arrived(1, 7)
    use(1, 6, 2)
    for kind, out in ((1, image_grad_ref), (0, text_grad_ref)):
        unit, inverse = normalize(kind)
        grad = acc[1 - kind]
        out[...] = inverse * (grad - unit * jnp.sum(unit * grad, axis=-1, keepdims=True))
    for one in started:
        one.wait_send()

    @pl.when(even == 0)
    def _():
        for one in started_if:
            one.wait_send()


def per_device(n_loop, n_grp, images, texts, log_scale, bias):
    rows, width = images.shape
    vmem = pl.BlockSpec(memory_space=pltpu.VMEM)
    smem = pl.BlockSpec(memory_space=pltpu.SMEM)
    hbm = pl.BlockSpec(memory_space=pl.ANY)
    grad = jax.ShapeDtypeStruct((rows, width), jnp.float32)
    dma = pltpu.SemaphoreType.DMA
    return pl.pallas_call(
        functools.partial(kernel, n_loop, n_grp),
        out_shape=(grad, grad),
        in_specs=[hbm, hbm, smem, smem],
        out_specs=(vmem, vmem),
        scratch_shapes=[
            pltpu.VMEM((2, rows, width), jnp.bfloat16),
            pltpu.VMEM((2, rows, width), jnp.bfloat16),
            pltpu.VMEM((2, rows, width), jnp.bfloat16),
            pltpu.VMEM((2, WIN - 1, rows, width), jnp.bfloat16),
            pltpu.VMEM((2, rows, width), jnp.float32),
            dma((2,)),
            dma((2, PARTS)),
            dma((2, PARTS)),
            dma((2, WIN - 1, PARTS)),
            dma((2, WIN - 1, PARTS)),
            dma((2, WIN - 1, PARTS)),
            dma((2, WIN - 1, PARTS)),
        ],
        compiler_params=pltpu.CompilerParams(
            collective_id=0, has_side_effects=True, vmem_limit_bytes=48 * 1024 * 1024
        ),
    )(
        *(pltpu.with_memory_space_constraint(value, pltpu.HBM) for value in (images, texts)),
        log_scale.reshape(1),
        bias.reshape(1),
    )


def solution(mesh):
    rows = P(("loop", "grp"), None)
    return jax.shard_map(
        functools.partial(per_device, mesh.shape["loop"], mesh.shape["grp"]),
        mesh=mesh,
        in_specs=(rows, rows, P(), P()),
        out_specs=(rows, rows),
        check_vma=False,
    )
```

```python
import functools

import jax
import jax.numpy as jnp
from jax import lax
from jax.experimental import pallas as pl
from jax.experimental.pallas import tpu as pltpu
from jax.sharding import PartitionSpec as P

WIN = 8
CHUNKS = 3
SIZES = (2, 2, 2, 2)
PARTS = len(SIZES)
ROUTES = ('CDDY', 'CDDY')
MESH = pl.DeviceIdType.MESH
NT = (((1,), (1,)), ((), ()))


def kernel(
    n_loop, n_grp, images_hbm, texts_hbm, log_scale_ref, bias_ref, image_grad_ref, text_grad_ref,
    raw, own, crossed, held, acc, load_sem, cross_send, cross_recv, send_sem, pass_sem, turn_sem, recv_sem,
):
    n = n_loop * n_grp
    wide = own.shape[2] // CHUNKS
    unit = images_hbm.shape[0] // 8
    offsets = [sum(SIZES[:h]) * unit for h in range(PARTS)]
    me = lax.axis_index("loop") * n_grp + lax.axis_index("grp")
    bits = [lax.rem(me, 2), lax.rem(me // 2, 2), lax.rem(me // 4, 2)]
    top = [None] + [bits[r.bit_length() - 1] for r in range(1, WIN)]

    def place(device):
        return (device // n_grp, lax.rem(device, n_grp))

    def member(r):
        device = me
        for b in range(3):
            if r >> b & 1:
                device = device + (1 - 2 * bits[b]) * (1 << b)
        return place(device)

    above, below = place(lax.rem(me + WIN, n)), place(lax.rem(me - WIN + n, n))
    loads = [
        pltpu.make_async_copy(ref, raw.at[i], load_sem.at[i]) for i, ref in enumerate((texts_hbm, images_hbm))
    ]
    for one in loads:
        one.start()
    barrier = pltpu.get_barrier_semaphore()
    peers = [above, below] + [member(r) for r in (1, 2, 4, 6)]
    for peer in peers:
        pl.semaphore_signal(barrier, inc=1, device_id=peer, device_id_type=MESH)

    def normalize(kind):
        full = raw[kind].astype(jnp.float32)
        inverse = lax.rsqrt(jnp.sum(full * full, axis=-1, keepdims=True) + 1e-06)
        return full * inverse, inverse

    inverses = []
    for kind in range(2):
        loads[kind].wait()
        unit_rows, inverse = normalize(kind)
        own[kind] = unit_rows.astype(jnp.bfloat16)
        inverses.append(inverse)
    pl.semaphore_wait(barrier, len(peers))

    def half(ref, h):
        return ref.at[pl.ds(offsets[h], SIZES[h] * unit)]

    def send(source, late, r, h, sem, device):
        return pltpu.make_async_remote_copy(
            src_ref=half(source, h), dst_ref=half(held.at[late, r - 1], h), send_sem=sem.at[late, r - 1, h],
            recv_sem=recv_sem.at[late, r - 1, h], device_id=device, device_id_type=MESH,
        )

    def cross(kind, h):
        return pltpu.make_async_remote_copy(
            src_ref=half(own.at[kind], h), dst_ref=half(crossed.at[kind], h), send_sem=cross_send.at[kind, h],
            recv_sem=cross_recv.at[kind, h], device_id=(above, below)[kind], device_id_type=MESH,
        )

    started = []

    def start(one):
        one.start()
        started.append(one)

    def spread(late, h):
        def block(r):
            return crossed.at[1 - top[r]] if late else own.at[top[r]]

        for r in (2, 4, 1):
            start(send(block(r), late, r, h, send_sem, member(r)))
        if ROUTES[late][h] == "C":
            start_if(send(block(6), late, 6, h, send_sem, member(6)))

    even = bits[1] * bits[2] + (1 - bits[1]) * (1 - bits[2])
    turn = place(me + even * (1 - 2 * bits[1]) * 2 + (1 - even) * (1 - 2 * bits[2]) * 4)
    started_if = []

    def start_if(one):
        @pl.when(even == 0)
        def _():
            one.start()

        started_if.append(one)

    def relay(late, h):
        route = ROUTES[late][h]
        if route == "Y":
            start(send(held.at[late, 3], late, 6, h, turn_sem, member(2)))
        elif route == "D":
            start(send(held.at[late, 1 + 2 * even], late, 6, h, turn_sem, turn))
        else:
            start_if(send(held.at[late, 1], late, 6, h, turn_sem, member(4)))

    def direct(late, h):
        for r in (2, 4):
            send(own.at[0], late, r, h, send_sem, member(1)).wait_recv()
        relay(late, h)
        for r in (2, 4):
            start(send(held.at[late, r - 1], late, r + 1, h, pass_sem, member(1)))

    scale = jnp.exp(jnp.full((1, 1), log_scale_ref[0], jnp.float32))
    bias = bias_ref[0]

    def step(kind, block, matched=False):
        def columns(ref, c):
            value = ref[..., c * wide : (c + 1) * wide]
            return value.reshape(-1, wide)

        logits = sum(
            lax.dot_general(columns(own.at[1 - kind], c), columns(block, c), NT, preferred_element_type=jnp.float32)
            for c in range(CHUNKS)
        )
        level = scale * logits + bias
        if matched:
            rows = lax.broadcasted_iota(jnp.int32, level.shape, 0)
            others = lax.broadcasted_iota(jnp.int32, level.shape, 1)
            sign = jnp.where(rows == others, 1.0, -1.0)
            weights = scale * -sign * jax.nn.sigmoid(-sign * level)
        else:
            weights = scale * jax.nn.sigmoid(level)
        weights = weights.astype(jnp.bfloat16)
        for c in range(CHUNKS):
            at = (kind, slice(None), slice(c * wide, (c + 1) * wide))
            part = jnp.dot(weights, columns(block, c), preferred_element_type=jnp.float32)
            acc[at] = part if matched else acc[at] + part

    for h in range(PARTS):
        for kind in range(2):
            start(cross(kind, h))
        spread(0, h)
    for kind in range(2):
        step(kind, own.at[kind], True)

    def arrived(late, *relations):
        for h in range(PARTS):
            for r in relations:
                send(own.at[0], late, r, h, send_sem, member(1)).wait_recv()
                if r == 6:
                    start(send(held.at[late, 5], late, 7, h, pass_sem, member(1)))

    def use(late, first, count):
        step(top[first] if late else 1 - top[first], held.at[late, pl.ds(first - 1, count)])

    def crossing(h):
        for kind in range(2):
            cross(kind, h).wait_recv()
        spread(1, h)

    arrived(0, 1)
    use(0, 1, 1)
    direct(0, 0)
    direct(0, 1)
    crossing(0)
    direct(0, 2)
    direct(0, 3)
    crossing(1)
    use(0, 2, 1)
    use(0, 4, 1)
    crossing(2)
    arrived(0, 3, 5)
    use(0, 3, 1)
    direct(1, 0)
    crossing(3)
    direct(1, 1)
    arrived(0, 6)
    direct(1, 2)
    use(0, 5, 1)
    direct(1, 3)
    arrived(1, 1)
    use(1, 1, 1)
    use(1, 2, 1)
    use(1, 4, 1)
    arrived(0, 7)
    use(0, 6, 2)
    arrived(1, 3, 5)
    arrived(1, 6)
    use(1, 3, 1)
    use(1, 5, 1)
    arrived(1, 7)
    use(1, 6, 2)
    for kind, out in ((1, image_grad_ref), (0, text_grad_ref)):
        inverse = inverses[kind]
        unit = raw[kind].astype(jnp.float32) * inverse
        grad = acc[1 - kind]
        out[...] = inverse * (grad - unit * jnp.sum(unit * grad, axis=-1, keepdims=True))
    for one in started:
        one.wait_send()

    @pl.when(even == 0)
    def _():
        for one in started_if:
            one.wait_send()


def per_device(n_loop, n_grp, images, texts, log_scale, bias):
    rows, width = images.shape
    vmem = pl.BlockSpec(memory_space=pltpu.VMEM)
    smem = pl.BlockSpec(memory_space=pltpu.SMEM)
    hbm = pl.BlockSpec(memory_space=pl.ANY)
    grad = jax.ShapeDtypeStruct((rows, width), jnp.float32)
    dma = pltpu.SemaphoreType.DMA
    return pl.pallas_call(
        functools.partial(kernel, n_loop, n_grp),
        out_shape=(grad, grad),
        in_specs=[hbm, hbm, smem, smem],
        out_specs=(vmem, vmem),
        scratch_shapes=[
            pltpu.VMEM((2, rows, width), jnp.bfloat16),
            pltpu.VMEM((2, rows, width), jnp.bfloat16),
            pltpu.VMEM((2, rows, width), jnp.bfloat16),
            pltpu.VMEM((2, WIN - 1, rows, width), jnp.bfloat16),
            pltpu.VMEM((2, rows, width), jnp.float32),
            dma((2,)),
            dma((2, PARTS)),
            dma((2, PARTS)),
            dma((2, WIN - 1, PARTS)),
            dma((2, WIN - 1, PARTS)),
            dma((2, WIN - 1, PARTS)),
            dma((2, WIN - 1, PARTS)),
        ],
        compiler_params=pltpu.CompilerParams(
            collective_id=0, has_side_effects=True, vmem_limit_bytes=48 * 1024 * 1024
        ),
    )(
        *(pltpu.with_memory_space_constraint(value, pltpu.HBM) for value in (images, texts)),
        log_scale.reshape(1),
        bias.reshape(1),
    )


def solution(mesh):
    rows = P(("loop", "grp"), None)
    return jax.shard_map(
        functools.partial(per_device, mesh.shape["loop"], mesh.shape["grp"]),
        mesh=mesh,
        in_specs=(rows, rows, P(), P()),
        out_specs=(rows, rows),
        check_vma=False,
    )
```
